32 devices in a mesh: blk: 8 (over z, x), freq: 4 (over y, core).
Axes of the slice: x: 2, y: 2, z: 4, core: 2. Of those that a mesh axis runs over, the one named last changes fastest.
Arguments:
- spectra: bfloat16 [2, 128, 1024, 512], P(None, 'freq', 'blk'), may hold values from -6 to 6
- halfwidth: int32 [1024], P('blk'), may hold values from 1 to 3
Outputs:
- cross: bfloat16 [2, 2, 128, 1024, 128], P(None, None, 'freq', 'blk')
The draws below stay inside these ranges and needn't reach their ends.
All inputs are finite; a program needn't handle non-finite values.
Results may differ from the reference program's by a relative error of at most 0.0064.
Values may be sent and summed in bfloat16 or wider, within the bound.
A program may use at most 128 MiB of HBM per device.

```python
import jax
import jax.numpy as jnp
from jax import lax

CB = 128
W = 512
F = 128
HMAX = 3
ROUNDS = 2
C = 1024
N_BLK = 8


def set_ends(array, rng, smallest, top_value):
    extent = array.shape
    index_at = [jax.random.randint(jax.random.fold_in(rng, axis), (), 0, extent[axis]) for axis in range(len(extent))]
    array = array.at[tuple(index_at)].set(smallest)
    longest = extent.index(max(extent))
    index_at[longest] = (index_at[longest] + 1) % extent[longest]
    return array.at[tuple(index_at)].set(top_value)


def shard_levels(key, dims, cuts, smallest, top_value):
    def one(axis_at, shards_of):
        heights = jax.random.uniform(jax.random.fold_in(jax.random.fold_in(key, 6), axis_at), (shards_of,), jnp.float32, smallest / len(cuts), top_value / len(cuts))
        return jnp.repeat(jnp.exp(heights), dims[axis_at] // shards_of).reshape((-1,) + (1,) * (len(dims) - axis_at - 1))

    loudness = one(*cuts[0])
    for cut in cuts[1:]:
        loudness = loudness * one(*cut)
    return loudness


def bell_draw(rng, extent, deviation, reach, pieces=(), kind=jnp.bfloat16):
    entries = deviation * jax.random.normal(rng, extent, jnp.float32)
    if pieces:
        entries = entries * shard_levels(rng, extent, pieces, -0.22, 0.18)
    return jnp.clip(entries, -reach, reach).astype(kind)


def setup_inputs(seed: int = 0) -> dict:
    splits = jax.random.split(jax.random.key(seed), 3)
    spectra = bell_draw(splits[0], (2, F, C, W), 1.0, 6.0, ((1, 4), (2, 8)))
    halfwidth = set_ends(jax.random.randint(splits[1], (C,), 1, HMAX + 1), jax.random.fold_in(splits[1], 1), 1, HMAX).astype(jnp.int32)
    return {"spectra": spectra, "halfwidth": halfwidth}


def whiten_all(block, widths):
    real_part = block[0].astype(jnp.float32)
    imag_part = block[1].astype(jnp.float32)
    energy = real_part * real_part + imag_part * imag_part
    padded = jnp.pad(energy, ((HMAX, HMAX), (0, 0), (0, 0)))
    bin_index = jnp.arange(F, dtype=jnp.int32)
    smooth = jnp.zeros_like(energy)
    counts = jnp.zeros((F, CB), jnp.float32)
    for offset in range(-HMAX, HMAX + 1):
        inside = abs(offset) <= widths
        in_grid = (bin_index + offset >= 0) & (bin_index + offset < F)
        weight = (inside[None, :] & in_grid[:, None]).astype(jnp.float32)
        smooth = smooth + weight[:, :, None] * padded[offset + HMAX:offset + HMAX + F]
        counts = counts + weight
    root_mean = jnp.sqrt(smooth / counts[:, :, None])
    factor = 1.0 / jnp.maximum(root_mean, 0.5)
    return jnp.stack((real_part * factor, imag_part * factor)).astype(jnp.bfloat16)

def cross_sums(own_block, partner):
    own_real = own_block[0].astype(jnp.float32)
    own_imag = own_block[1].astype(jnp.float32)
    par_real = partner[0].astype(jnp.float32)
    par_imag = partner[1].astype(jnp.float32)
    real_sum = jnp.einsum('fcw,fdw->fcd', own_real, par_real) + jnp.einsum('fcw,fdw->fcd', own_imag, par_imag)
    imag_sum = jnp.einsum('fcw,fdw->fcd', own_imag, par_real) - jnp.einsum('fcw,fdw->fcd', own_real, par_imag)
    return jnp.stack((real_sum, imag_sum)).astype(jnp.bfloat16)

def reference(spectra, halfwidth):
    blocks = jnp.moveaxis(spectra.reshape(2, F, N_BLK, CB, W), 2, 0)
    widths = halfwidth.reshape(N_BLK, CB)
    whitened = lax.map(lambda pair: whiten_all(pair[0], pair[1]), (blocks, widths))
    half_len = W // 2
    tile_list = []
    for round_index in range(ROUNDS):
        flip = N_BLK >> round_index + 1

        def single(index):
            own_block = whitened[index]
            partner = whitened[index ^ flip]
            first = cross_sums(own_block[..., :half_len], partner[..., :half_len])
            second = cross_sums(own_block[..., half_len:], partner[..., half_len:])
            summed = first.astype(jnp.float32) + second.astype(jnp.float32)
            return (summed * W ** (-0.5)).astype(jnp.bfloat16)
        tiles = lax.map(single, jnp.arange(N_BLK, dtype=jnp.int32))
        tile_list.append(jnp.moveaxis(tiles, 0, 2).reshape(2, F, N_BLK * CB, CB))
    return jnp.stack(tile_list)
```

```python
import jax
import jax.numpy as jnp
from jax import lax
from jax.experimental import pallas as pl
from jax.experimental.pallas import tpu as pltpu
from jax.sharding import PartitionSpec as P

HMAX = 3
ROUNDS = 2
STEP = 2
ROWS = 16
LANES = 128


def cross_kernel(
    spectra, widths, out, energy, whitened, taken, own_tiles, sent_tiles,
    halo_send, halo_recv, x_send, x_recv, t_send, t_recv, o_sem,
):
    _, bins, channels, windows = spectra.shape
    half = bins // 2
    chunks = half // STEP
    fresh_chunks = (half - 2 * HMAX) // STEP
    first_edge_chunk = (half - HMAX) // STEP
    row_blocks = channels // ROWS
    scale = windows ** -0.5

    block = lax.axis_index("blk")
    block_count = lax.axis_size("blk")
    freq = lax.axis_index("freq")
    freq_count = lax.axis_size("freq")
    bin_total = bins * freq_count
    has_low = freq > 0
    has_high = freq < freq_count - 1

    partners = []
    mine = 0
    for round_index in range(ROUNDS):
        flip = block_count >> (round_index + 1)
        side = (block // flip) % 2
        partners.append(block + flip * (1 - 2 * side))
        mine = mine + side
    mine = mine % 2
    given = 1 - mine

    def chunk_start(which, chunk):
        return (half - STEP * (chunk + 1)) + which * (STEP * (2 * chunk + 1))

    def make_energy(k):
        @pl.loop(0, row_blocks)
        def _(block_index):
            rows = pl.ds(pl.multiple_of(block_index * ROWS, ROWS), ROWS)
            real_part = spectra[0, k, rows, :].astype(jnp.float32)
            imag_part = spectra[1, k, rows, :].astype(jnp.float32)
            energy[k + HMAX, rows, :] = real_part * real_part + imag_part * imag_part

    def whiten(k):
        position = freq * bins + k
        inside = []
        for offset in range(1, HMAX + 1):
            low = (position - offset >= 0).astype(jnp.int32)
            high = (position + offset < bin_total).astype(jnp.int32)
            inside.append((low + high).astype(jnp.float32))

        @pl.loop(0, row_blocks)
        def _(block_index):
            rows = pl.ds(pl.multiple_of(block_index * ROWS, ROWS), ROWS)
            width = widths[rows, :]
            counts = jnp.ones((ROWS, LANES), jnp.float32)
            weights = []
            for offset in range(1, HMAX + 1):
                weight = (width >= offset).astype(jnp.float32)
                counts = counts + weight * inside[offset - 1]
                weights.append(weight)
            inverse = 1.0 / counts
            for lane in range(0, windows, LANES):
                lanes = pl.ds(lane, LANES)
                smooth = energy[k + HMAX, rows, lanes]
                for offset in range(1, HMAX + 1):
                    pair = (
                        energy[k + HMAX - offset, rows, lanes]
                        + energy[k + HMAX + offset, rows, lanes]
                    )
                    smooth = smooth + weights[offset - 1] * pair
                factor = lax.rsqrt(jnp.maximum(smooth * inverse, 0.25))
                for part in range(2):
                    value = spectra[part, k, rows, lanes].astype(jnp.float32)
                    whitened[part, k, rows, lanes] = (value * factor).astype(jnp.bfloat16)

    def halo_copy(side):
        source = (HMAX, bins)[side]
        target = (bins + HMAX, 0)[side]
        return pltpu.make_async_remote_copy(
            src_ref=energy.at[pl.ds(source, HMAX)],
            dst_ref=energy.at[pl.ds(target, HMAX)],
            send_sem=halo_send.at[side],
            recv_sem=halo_recv.at[1 - side],
            device_id={"freq": freq + (2 * side - 1)},
            device_id_type=pl.DeviceIdType.MESH,
        )

    def spectra_copy(r, chunk):
        return pltpu.make_async_remote_copy(
            src_ref=whitened.at[:, pl.ds(chunk_start(given, chunk), STEP)],
            dst_ref=taken.at[r, :, pl.ds(chunk * STEP, STEP)],
            send_sem=x_send.at[r, chunk],
            recv_sem=x_recv.at[r, chunk],
            device_id={"blk": partners[r]},
            device_id_type=pl.DeviceIdType.MESH,
        )

    def tile_copy(r, chunk, which):
        return pltpu.make_async_remote_copy(
            src_ref=sent_tiles.at[r, chunk],
            dst_ref=out.at[r, :, pl.ds(chunk_start(which, chunk), STEP)],
            send_sem=t_send.at[r, chunk],
            recv_sem=t_recv.at[r, chunk],
            device_id={"blk": partners[r]},
            device_id_type=pl.DeviceIdType.MESH,
        )

    def own_copy(r, chunk):
        return pltpu.make_async_copy(
            own_tiles.at[r, chunk],
            out.at[r, :, pl.ds(chunk_start(mine, chunk), STEP)],
            o_sem.at[r, chunk],
        )

    barrier = pltpu.get_barrier_semaphore()
    for partner in partners:
        pl.semaphore_signal(
            barrier, inc=1, device_id={"blk": partner}, device_id_type=pl.DeviceIdType.MESH
        )

    @pl.when(has_low)
    def _():
        pl.semaphore_signal(
            barrier, inc=1, device_id={"freq": freq - 1}, device_id_type=pl.DeviceIdType.MESH
        )

    @pl.when(has_high)
    def _():
        pl.semaphore_signal(
            barrier, inc=1, device_id={"freq": freq + 1}, device_id_type=pl.DeviceIdType.MESH
        )

    @pl.loop(0, HMAX)
    def _(index):
        make_energy(index)
        make_energy(bins - HMAX + index)

    pl.semaphore_wait(barrier, ROUNDS + has_low.astype(jnp.int32) + has_high.astype(jnp.int32))

    @pl.when(has_low)
    def _():
        halo_copy(0).start()

    @pl.when(jnp.logical_not(has_low))
    def _():
        energy[pl.ds(0, HMAX)] = jnp.zeros((HMAX, channels, windows), jnp.float32)

    @pl.when(has_high)
    def _():
        halo_copy(1).start()

    @pl.when(jnp.logical_not(has_high))
    def _():
        energy[pl.ds(bins + HMAX, HMAX)] = jnp.zeros((HMAX, channels, windows), jnp.float32)

    @pl.loop(half - HMAX, half + HMAX)
    def _(index):
        make_energy(index)

    def whiten_half(which, send):
        @pl.loop(0, chunks)
        def _(chunk):
            start = chunk_start(which, chunk)

            @pl.when(chunk < fresh_chunks)
            def _():
                for j in range(STEP):
                    make_energy(start + j + HMAX * (2 * which - 1))

            @pl.when((chunk == first_edge_chunk) & (which == 0) & has_low)
            def _():
                halo_copy(1).wait_recv()

            @pl.when((chunk == first_edge_chunk) & (which == 1) & has_high)
            def _():
                halo_copy(0).wait_recv()

            @pl.loop(0, STEP)
            def _(j):
                whiten(start + j)

            if send:
                for r in range(ROUNDS):
                    spectra_copy(r, chunk).start()

    whiten_half(given, True)
    whiten_half(mine, False)

    @pl.loop(0, chunks)
    def _(chunk):
        start = chunk_start(mine, chunk)
        for r in range(ROUNDS):
            spectra_copy(r, chunk).wait_recv()

            @pl.loop(0, STEP)
            def _(j):
                own = jnp.concatenate([whitened[0, start + j], whitened[1, start + j]], axis=0)
                other = jnp.concatenate(
                    [taken[r, 0, chunk * STEP + j], taken[r, 1, chunk * STEP + j]], axis=0
                )
                both = lax.dot_general(
                    own, other, (((1,), (1,)), ((), ())), preferred_element_type=jnp.float32
                )
                real_sum = both[:channels, :channels] + both[channels:, channels:]
                imag_sum = both[channels:, :channels] - both[:channels, channels:]
                real_sum = real_sum * scale
                imag_sum = imag_sum * scale
                own_tiles[r, chunk, 0, j] = real_sum.astype(jnp.bfloat16)
                own_tiles[r, chunk, 1, j] = imag_sum.astype(jnp.bfloat16)
                sent_tiles[r, chunk, 0, j] = real_sum.T.astype(jnp.bfloat16)
                sent_tiles[r, chunk, 1, j] = (-imag_sum.T).astype(jnp.bfloat16)

            tile_copy(r, chunk, mine).start()
            own_copy(r, chunk).start()

    @pl.when(has_low)
    def _():
        halo_copy(0).wait_send()

    @pl.when(has_high)
    def _():
        halo_copy(1).wait_send()

    @pl.loop(0, chunks)
    def _(chunk):
        for r in range(ROUNDS):
            spectra_copy(r, chunk).wait_send()
            own_copy(r, chunk).wait()
            tile_copy(r, chunk, mine).wait_send()
            tile_copy(r, chunk, given).wait_recv()


def per_device(spectra, halfwidth):
    _, bins, channels, windows = spectra.shape
    half = bins // 2
    chunks = half // STEP
    widths = jnp.broadcast_to(halfwidth[:, None], (channels, LANES))
    tiles = (ROUNDS, chunks, 2, STEP, channels, channels)
    dma = pltpu.SemaphoreType.DMA
    return pl.pallas_call(
        cross_kernel,
        out_shape=jax.ShapeDtypeStruct((ROUNDS, 2, bins, channels, channels), jnp.bfloat16),
        in_specs=[pl.BlockSpec(memory_space=pltpu.VMEM)] * 2,
        out_specs=pl.BlockSpec(memory_space=pl.ANY),
        scratch_shapes=[
            pltpu.VMEM((bins + 2 * HMAX, channels, windows), jnp.float32),
            pltpu.VMEM((2, bins, channels, windows), jnp.bfloat16),
            pltpu.VMEM((ROUNDS, 2, half, channels, windows), jnp.bfloat16),
            pltpu.VMEM(tiles, jnp.bfloat16),
            pltpu.VMEM(tiles, jnp.bfloat16),
            dma((2,)),
            dma((2,)),
            dma((ROUNDS, chunks)),
            dma((ROUNDS, chunks)),
            dma((ROUNDS, chunks)),
            dma((ROUNDS, chunks)),
            dma((ROUNDS, chunks)),
        ],
        compiler_params=pltpu.CompilerParams(
            collective_id=0, has_side_effects=True, vmem_limit_bytes=56 * 2**20
        ),
    )(spectra, widths)


def solution(mesh):
    return jax.shard_map(
        per_device,
        mesh=mesh,
        in_specs=(P(None, "freq", "blk", None), P("blk")),
        out_specs=P(None, None, "freq", "blk", None),
        check_vma=False,
    )
```

```python
import jax
import jax.numpy as jnp
from jax import lax
from jax.experimental import pallas as pl
from jax.experimental.pallas import tpu as pltpu
from jax.sharding import PartitionSpec as P

HMAX = 3
ROUNDS = 2
STEP = 1
ROWS = 16
LANES = 128


def cross_kernel(
    spectra_in, widths_in, out, spectra, widths, energy, whitened, taken, sent_tiles,
    in_sem, halo_send, halo_recv, x_send, x_recv, t_send, t_recv,
):
    _, bins, channels, windows = spectra.shape
    half = bins // 2
    middle = HMAX + STEP
    chunks = half // STEP
    fresh_chunks = (half - 2 * HMAX) // STEP
    first_edge_chunk = (half - HMAX) // STEP
    row_blocks = channels // ROWS
    scale = windows ** -0.5

    block = lax.axis_index("blk")
    block_count = lax.axis_size("blk")
    freq = lax.axis_index("freq")
    freq_count = lax.axis_size("freq")
    bin_total = bins * freq_count
    has_low = freq > 0
    has_high = freq < freq_count - 1

    partners = []
    mine = 0
    for round_index in range(ROUNDS):
        flip = block_count >> (round_index + 1)
        side = (block // flip) % 2
        partners.append(block + flip * (1 - 2 * side))
        mine = mine + side
    mine = mine % 2
    given = 1 - mine

    def chunk_start(which, chunk):
        return (half - STEP * (chunk + 1)) + which * (STEP * (2 * chunk + 1))

    def make_energy(k):
        @pl.loop(0, row_blocks)
        def _(block_index):
            rows = pl.ds(pl.multiple_of(block_index * ROWS, ROWS), ROWS)
            real_part = spectra[0, k, rows, :].astype(jnp.float32)
            imag_part = spectra[1, k, rows, :].astype(jnp.float32)
            energy[k + HMAX, rows, :] = real_part * real_part + imag_part * imag_part

    def whiten(k):
        position = freq * bins + k
        inside = []
        for offset in range(1, HMAX + 1):
            low = (position - offset >= 0).astype(jnp.int32)
            high = (position + offset < bin_total).astype(jnp.int32)
            inside.append((low + high).astype(jnp.float32))

        @pl.loop(0, row_blocks)
        def _(block_index):
            rows = pl.ds(pl.multiple_of(block_index * ROWS, ROWS), ROWS)
            width = widths[rows, :]
            counts = jnp.ones((ROWS, LANES), jnp.float32)
            weights = []
            for offset in range(1, HMAX + 1):
                weight = (width >= offset).astype(jnp.float32)
                counts = counts + weight * inside[offset - 1]
                weights.append(weight)
            inverse = 1.0 / counts
            for lane in range(0, windows, LANES):
                lanes = pl.ds(lane, LANES)
                smooth = energy[k + HMAX, rows, lanes]
                for offset in range(1, HMAX + 1):
                    pair = (
                        energy[k + HMAX - offset, rows, lanes]
                        + energy[k + HMAX + offset, rows, lanes]
                    )
                    smooth = smooth + weights[offset - 1] * pair
                factor = lax.rsqrt(jnp.maximum(smooth * inverse, 0.25))
                for part in range(2):
                    value = spectra[part, k, rows, lanes].astype(jnp.float32)
                    whitened[part, k, rows, lanes] = (value * factor).astype(jnp.bfloat16)

    def halo_copy(side):
        source = (HMAX, bins)[side]
        target = (bins + HMAX, 0)[side]
        return pltpu.make_async_remote_copy(
            src_ref=energy.at[pl.ds(source, HMAX)],
            dst_ref=energy.at[pl.ds(target, HMAX)],
            send_sem=halo_send.at[side],
            recv_sem=halo_recv.at[1 - side],
            device_id={"freq": freq + (2 * side - 1)},
            device_id_type=pl.DeviceIdType.MESH,
        )

    def spectra_copy(r, chunk):
        return pltpu.make_async_remote_copy(
            src_ref=whitened.at[:, pl.ds(chunk_start(given, chunk), STEP)],
            dst_ref=taken.at[r, :, pl.ds(chunk * STEP, STEP)],
            send_sem=x_send.at[r, chunk],
            recv_sem=x_recv.at[r, chunk],
            device_id={"blk": partners[r]},
            device_id_type=pl.DeviceIdType.MESH,
        )

    def tile_copy(r, chunk, which):
        return pltpu.make_async_remote_copy(
            src_ref=sent_tiles.at[r, chunk],
            dst_ref=out.at[r, :, pl.ds(chunk_start(which, chunk), STEP)],
            send_sem=t_send.at[r, chunk],
            recv_sem=t_recv.at[r, chunk],
            device_id={"blk": partners[r]},
            device_id_type=pl.DeviceIdType.MESH,
        )

    def load(start, count, index):
        span = pl.ds(start, count)
        return pltpu.make_async_copy(spectra_in.at[:, span], spectra.at[:, span], in_sem.at[index])

    loads = (
        load(half - middle, 2 * middle, 0),
        load(given * (half + middle), half - middle, 1),
        load(mine * (half + middle), half - middle, 2),
    )
    for copy in loads:
        copy.start()

    barrier = pltpu.get_barrier_semaphore()
    for partner in partners:
        pl.semaphore_signal(
            barrier, inc=1, device_id={"blk": partner}, device_id_type=pl.DeviceIdType.MESH
        )

    @pl.when(has_low)
    def _():
        pl.semaphore_signal(
            barrier, inc=1, device_id={"freq": freq - 1}, device_id_type=pl.DeviceIdType.MESH
        )

    @pl.when(has_high)
    def _():
        pl.semaphore_signal(
            barrier, inc=1, device_id={"freq": freq + 1}, device_id_type=pl.DeviceIdType.MESH
        )

    widths[...] = jnp.broadcast_to(
        widths_in[...].astype(jnp.float32), (channels, LANES)
    ).T

    loads[0].wait()

    @pl.loop(half - HMAX, half + HMAX)
    def _(index):
        make_energy(index)

    def whiten_chunk(which, chunk):
        start = chunk_start(which, chunk)

        @pl.when(chunk < fresh_chunks)
        def _():
            for j in range(STEP):
                make_energy(start + j + HMAX * (2 * which - 1))

        @pl.when((chunk == first_edge_chunk) & (which == 0) & has_low)
        def _():
            halo_copy(1).wait_recv()

        @pl.when((chunk == first_edge_chunk) & (which == 1) & has_high)
        def _():
            halo_copy(0).wait_recv()

        for j in range(STEP):
            whiten(start + j)

    def give(chunk):
        for r in range(ROUNDS):
            spectra_copy(r, chunk).start()

    whiten_chunk(given, 0)
    pl.semaphore_wait(barrier, ROUNDS + has_low.astype(jnp.int32) + has_high.astype(jnp.int32))
    give(0)

    loads[1].wait()
    loads[2].wait()

    @pl.loop(0, HMAX)
    def _(index):
        make_energy(index)
        make_energy(bins - HMAX + index)

    @pl.when(has_low)
    def _():
        halo_copy(0).start()

    @pl.when(jnp.logical_not(has_low))
    def _():
        energy[pl.ds(0, HMAX)] = jnp.zeros((HMAX, channels, windows), jnp.float32)

    @pl.when(has_high)
    def _():
        halo_copy(1).start()

    @pl.when(jnp.logical_not(has_high))
    def _():
        energy[pl.ds(bins + HMAX, HMAX)] = jnp.zeros((HMAX, channels, windows), jnp.float32)

    @pl.loop(1, chunks)
    def _(chunk):
        whiten_chunk(given, chunk)
        give(chunk)

    @pl.loop(0, chunks)
    def _(chunk):
        whiten_chunk(mine, chunk)

    @pl.loop(0, chunks)
    def _(chunk):
        start = chunk_start(mine, chunk)
        for r in range(ROUNDS):
            spectra_copy(r, chunk).wait_recv()

            @pl.loop(0, STEP)
            def _(j):
                own = jnp.concatenate([whitened[0, start + j], whitened[1, start + j]], axis=0)
                other = jnp.concatenate(
                    [taken[r, 0, chunk * STEP + j], taken[r, 1, chunk * STEP + j]], axis=0
                )
                both = lax.dot_general(
                    own, other, (((1,), (1,)), ((), ())), preferred_element_type=jnp.float32
                )
                real_sum = both[:channels, :channels] + both[channels:, channels:]
                imag_sum = both[channels:, :channels] - both[:channels, channels:]
                real_sum = real_sum * scale
                imag_sum = imag_sum * scale
                out[r, 0, start + j] = real_sum.astype(jnp.bfloat16)
                out[r, 1, start + j] = imag_sum.astype(jnp.bfloat16)
                sent_tiles[r, chunk, 0, j] = real_sum.T.astype(jnp.bfloat16)
                sent_tiles[r, chunk, 1, j] = (-imag_sum.T).astype(jnp.bfloat16)

            tile_copy(r, chunk, mine).start()

    @pl.when(has_low)
    def _():
        halo_copy(0).wait_send()

    @pl.when(has_high)
    def _():
        halo_copy(1).wait_send()

    @pl.loop(0, chunks)
    def _(chunk):
        for r in range(ROUNDS):
            spectra_copy(r, chunk).wait_send()
            tile_copy(r, chunk, mine).wait_send()
            tile_copy(r, chunk, given).wait_recv()


def per_device(spectra, halfwidth):
    _, bins, channels, windows = spectra.shape
    half = bins // 2
    chunks = half // STEP
    widths = halfwidth.reshape(1, channels)
    tiles = (ROUNDS, chunks, 2, STEP, channels, channels)
    dma = pltpu.SemaphoreType.DMA
    return pl.pallas_call(
        cross_kernel,
        out_shape=pltpu.VMEM((ROUNDS, 2, bins, channels, channels), jnp.bfloat16),
        in_specs=[
            pl.BlockSpec(memory_space=pltpu.HBM),
            pl.BlockSpec(memory_space=pltpu.VMEM),
        ],
        out_specs=pl.BlockSpec(memory_space=pltpu.VMEM),
        scratch_shapes=[
            pltpu.VMEM((2, bins, channels, windows), jnp.bfloat16),
            pltpu.VMEM((channels, LANES), jnp.float32),
            pltpu.VMEM((bins + 2 * HMAX, channels, windows), jnp.float32),
            pltpu.VMEM((2, bins, channels, windows), jnp.bfloat16),
            pltpu.VMEM((ROUNDS, 2, half, channels, windows), jnp.bfloat16),
            pltpu.VMEM(tiles, jnp.bfloat16),
            dma((3,)),
            dma((2,)),
            dma((2,)),
            dma((ROUNDS, chunks)),
            dma((ROUNDS, chunks)),
            dma((ROUNDS, chunks)),
            dma((ROUNDS, chunks)),
        ],
        compiler_params=pltpu.CompilerParams(
            collective_id=0, has_side_effects=True, vmem_limit_bytes=48 * 2**20
        ),
    )(spectra, widths)


def solution(mesh):
    return jax.shard_map(
        per_device,
        mesh=mesh,
        in_specs=(P(None, "freq", "blk", None), P("blk")),
        out_specs=P(None, None, "freq", "blk", None),
        check_vma=False,
    )
```

```python
import jax
import jax.numpy as jnp
from jax import lax
from jax.experimental import pallas as pl
from jax.experimental.pallas import tpu as pltpu
from jax.sharding import PartitionSpec as P

HMAX = 3
ROUNDS = 2
STEP = 2
PIECES = 4
ROWS = 16
LANES = 128


def cross_kernel(
    spectra_in, widths_in, out, spectra, widths, energy, whitened, taken, sent_tiles,
    in_sem, halo_send, halo_recv, x_send, x_recv, t_send, t_recv,
):
    _, bins, channels, windows = spectra.shape
    half = bins // 2
    middle = HMAX + STEP
    chunks = half // STEP
    fresh_chunks = (half - 2 * HMAX) // STEP
    first_edge_chunk = (half - HMAX) // STEP
    row_blocks = channels // ROWS
    scale = windows ** -0.5

    block = lax.axis_index("blk")
    block_count = lax.axis_size("blk")
    freq = lax.axis_index("freq")
    freq_count = lax.axis_size("freq")
    bin_total = bins * freq_count
    has_low = freq > 0
    has_high = freq < freq_count - 1

    partners = []
    mine = 0
    for round_index in range(ROUNDS):
        flip = block_count >> (round_index + 1)
        side = (block // flip) % 2
        partners.append(block + flip * (1 - 2 * side))
        mine = mine + side
    mine = mine % 2
    given = 1 - mine

    def chunk_start(which, chunk):
        return (half - STEP * (chunk + 1)) + which * (STEP * (2 * chunk + 1))

    def make_energy(k, first=0, last=row_blocks):
        @pl.loop(first, last)
        def _(block_index):
            rows = pl.ds(pl.multiple_of(block_index * ROWS, ROWS), ROWS)
            real_part = spectra[0, k, rows, :].astype(jnp.float32)
            imag_part = spectra[1, k, rows, :].astype(jnp.float32)
            energy[k + HMAX, rows, :] = real_part * real_part + imag_part * imag_part

    def whiten(k, first=0, last=row_blocks):
        position = freq * bins + k
        inside = []
        for offset in range(1, HMAX + 1):
            low = (position - offset >= 0).astype(jnp.int32)
            high = (position + offset < bin_total).astype(jnp.int32)
            inside.append((low + high).astype(jnp.float32))

        @pl.loop(first, last)
        def _(block_index):
            rows = pl.ds(pl.multiple_of(block_index * ROWS, ROWS), ROWS)
            width = widths[rows, :]
            counts = jnp.ones((ROWS, LANES), jnp.float32)
            weights = []
            for offset in range(1, HMAX + 1):
                weight = (width >= offset).astype(jnp.float32)
                counts = counts + weight * inside[offset - 1]
                weights.append(weight)
            inverse = 1.0 / counts
            for lane in range(0, windows, LANES):
                lanes = pl.ds(lane, LANES)
                smooth = energy[k + HMAX, rows, lanes]
                for offset in range(1, HMAX + 1):
                    pair = (
                        energy[k + HMAX - offset, rows, lanes]
                        + energy[k + HMAX + offset, rows, lanes]
                    )
                    smooth = smooth + weights[offset - 1] * pair
                factor = lax.rsqrt(jnp.maximum(smooth * inverse, 0.25))
                for part in range(2):
                    value = spectra[part, k, rows, lanes].astype(jnp.float32)
                    whitened[part, k, rows, lanes] = (value * factor).astype(jnp.bfloat16)

    def halo_copy(side):
        source = (HMAX, bins)[side]
        target = (bins + HMAX, 0)[side]
        return pltpu.make_async_remote_copy(
            src_ref=energy.at[pl.ds(source, HMAX)],
            dst_ref=energy.at[pl.ds(target, HMAX)],
            send_sem=halo_send.at[side],
            recv_sem=halo_recv.at[1 - side],
            device_id={"freq": freq + (2 * side - 1)},
            device_id_type=pl.DeviceIdType.MESH,
        )

    def spectra_copy(r, chunk, rows=pl.ds(0, channels)):
        return pltpu.make_async_remote_copy(
            src_ref=whitened.at[:, pl.ds(chunk_start(given, chunk), STEP), rows],
            dst_ref=taken.at[r, :, pl.ds(chunk * STEP, STEP), rows],
            send_sem=x_send.at[r, chunk],
            recv_sem=x_recv.at[r, chunk],
            device_id={"blk": partners[r]},
            device_id_type=pl.DeviceIdType.MESH,
        )

    def tile_copy(r, chunk, which):
        return pltpu.make_async_remote_copy(
            src_ref=sent_tiles.at[r, chunk],
            dst_ref=out.at[r, :, pl.ds(chunk_start(which, chunk), STEP)],
            send_sem=t_send.at[r, chunk],
            recv_sem=t_recv.at[r, chunk],
            device_id={"blk": partners[r]},
            device_id_type=pl.DeviceIdType.MESH,
        )

    def load(start, count, index, rows=pl.ds(0, channels)):
        span = pl.ds(start, count)
        return pltpu.make_async_copy(
            spectra_in.at[:, span, rows], spectra.at[:, span, rows], in_sem.at[index]
        )

    def piece_rows(piece):
        return pl.ds(pl.multiple_of(piece * (channels // PIECES), ROWS), channels // PIECES)

    def load_piece(piece):
        return load(half - middle, 2 * middle, piece, piece_rows(piece))

    for piece in range(PIECES):
        load_piece(piece).start()
    load_given = load(given * (half + middle), half - middle, PIECES)
    load_mine = load(mine * (half + middle), half - middle, PIECES + 1)
    load_given.start()
    load_mine.start()

    barrier = pltpu.get_barrier_semaphore()
    for partner in partners:
        pl.semaphore_signal(
            barrier, inc=1, device_id={"blk": partner}, device_id_type=pl.DeviceIdType.MESH
        )

    @pl.when(has_low)
    def _():
        pl.semaphore_signal(
            barrier, inc=1, device_id={"freq": freq - 1}, device_id_type=pl.DeviceIdType.MESH
        )

    @pl.when(has_high)
    def _():
        pl.semaphore_signal(
            barrier, inc=1, device_id={"freq": freq + 1}, device_id_type=pl.DeviceIdType.MESH
        )

    widths[...] = jnp.broadcast_to(
        widths_in[...].astype(jnp.float32), (channels, LANES)
    ).T

    def whiten_chunk(which, chunk):
        start = chunk_start(which, chunk)

        @pl.when(chunk < fresh_chunks)
        def _():
            for j in range(STEP):
                make_energy(start + j + HMAX * (2 * which - 1))

        @pl.when((chunk == first_edge_chunk) & (which == 0) & has_low)
        def _():
            halo_copy(1).wait_recv()

        @pl.when((chunk == first_edge_chunk) & (which == 1) & has_high)
        def _():
            halo_copy(0).wait_recv()

        for j in range(STEP):
            whiten(start + j)

    def give(chunk):
        for r in range(ROUNDS):
            spectra_copy(r, chunk).start()

    def first_piece(piece):
        first = piece * (row_blocks // PIECES)
        last = first + row_blocks // PIECES
        load_piece(piece).wait()

        @pl.loop(0, 2 * HMAX + STEP)
        def _(index):
            make_energy(half - HMAX - STEP * (1 - given) + index, first, last)

        for j in range(STEP):
            whiten(chunk_start(given, 0) + j, first, last)

    def give_piece(piece):
        for r in range(ROUNDS):
            spectra_copy(r, 0, piece_rows(piece)).start()

    first_piece(0)
    pl.semaphore_wait(barrier, ROUNDS + has_low.astype(jnp.int32) + has_high.astype(jnp.int32))
    give_piece(0)

    @pl.loop(1, PIECES)
    def _(piece):
        first_piece(piece)
        give_piece(piece)

    load_given.wait()
    load_mine.wait()

    @pl.loop(0, HMAX)
    def _(index):
        make_energy(index)
        make_energy(bins - HMAX + index)

    @pl.when(has_low)
    def _():
        halo_copy(0).start()

    @pl.when(jnp.logical_not(has_low))
    def _():
        energy[pl.ds(0, HMAX)] = jnp.zeros((HMAX, channels, windows), jnp.float32)

    @pl.when(has_high)
    def _():
        halo_copy(1).start()

    @pl.when(jnp.logical_not(has_high))
    def _():
        energy[pl.ds(bins + HMAX, HMAX)] = jnp.zeros((HMAX, channels, windows), jnp.float32)

    @pl.loop(1, chunks)
    def _(chunk):
        whiten_chunk(given, chunk)
        give(chunk)

    @pl.loop(0, chunks)
    def _(chunk):
        whiten_chunk(mine, chunk)

    @pl.loop(0, chunks)
    def _(chunk):
        start = chunk_start(mine, chunk)
        for r in range(ROUNDS):
            spectra_copy(r, chunk).wait_recv()

            @pl.loop(0, STEP)
            def _(j):
                own = jnp.concatenate([whitened[0, start + j], whitened[1, start + j]], axis=0)
                other = jnp.concatenate(
                    [taken[r, 0, chunk * STEP + j], taken[r, 1, chunk * STEP + j]], axis=0
                )
                both = lax.dot_general(
                    own, other, (((1,), (1,)), ((), ())), preferred_element_type=jnp.float32
                )
                real_sum = both[:channels, :channels] + both[channels:, channels:]
                imag_sum = both[channels:, :channels] - both[:channels, channels:]
                real_sum = real_sum * scale
                imag_sum = imag_sum * scale
                out[r, 0, start + j] = real_sum.astype(jnp.bfloat16)
                out[r, 1, start + j] = imag_sum.astype(jnp.bfloat16)
                sent_tiles[r, chunk, 0, j] = real_sum.T.astype(jnp.bfloat16)
                sent_tiles[r, chunk, 1, j] = (-imag_sum.T).astype(jnp.bfloat16)

            tile_copy(r, chunk, mine).start()

    @pl.when(has_low)
    def _():
        halo_copy(0).wait_send()

    @pl.when(has_high)
    def _():
        halo_copy(1).wait_send()

    @pl.loop(0, chunks)
    def _(chunk):
        for r in range(ROUNDS):
            spectra_copy(r, chunk).wait_send()
            tile_copy(r, chunk, mine).wait_send()
            tile_copy(r, chunk, given).wait_recv()


def per_device(spectra, halfwidth):
    _, bins, channels, windows = spectra.shape
    half = bins // 2
    chunks = half // STEP
    widths = halfwidth.reshape(1, channels)
    tiles = (ROUNDS, chunks, 2, STEP, channels, channels)
    dma = pltpu.SemaphoreType.DMA
    return pl.pallas_call(
        cross_kernel,
        out_shape=pltpu.VMEM((ROUNDS, 2, bins, channels, channels), jnp.bfloat16),
        in_specs=[
            pl.BlockSpec(memory_space=pltpu.HBM),
            pl.BlockSpec(memory_space=pltpu.VMEM),
        ],
        out_specs=pl.BlockSpec(memory_space=pltpu.VMEM),
        scratch_shapes=[
            pltpu.VMEM((2, bins, channels, windows), jnp.bfloat16),
            pltpu.VMEM((channels, LANES), jnp.float32),
            pltpu.VMEM((bins + 2 * HMAX, channels, windows), jnp.float32),
            pltpu.VMEM((2, bins, channels, windows), jnp.bfloat16),
            pltpu.VMEM((ROUNDS, 2, half, channels, windows), jnp.bfloat16),
            pltpu.VMEM(tiles, jnp.bfloat16),
            dma((PIECES + 2,)),
            dma((2,)),
            dma((2,)),
            dma((ROUNDS, chunks)),
            dma((ROUNDS, chunks)),
            dma((ROUNDS, chunks)),
            dma((ROUNDS, chunks)),
        ],
        compiler_params=pltpu.CompilerParams(
            collective_id=0, has_side_effects=True, vmem_limit_bytes=48 * 2**20
        ),
    )(spectra, widths)


def solution(mesh):
    return jax.shard_map(
        per_device,
        mesh=mesh,
        in_specs=(P(None, "freq", "blk", None), P("blk")),
        out_specs=P(None, None, "freq", "blk", None),
        check_vma=False,
    )
```

```python
import jax
import jax.numpy as jnp
from jax import lax
from jax.experimental import pallas as pl
from jax.experimental.pallas import tpu as pltpu
from jax.sharding import PartitionSpec as P

HMAX = 3
ROUNDS = 2
STEP = 2
PIECES = 8
ROWS = 16
LANES = 128


def cross_kernel(
    spectra_in, widths_in, out, spectra, widths, energy, whitened, taken, sent_tiles,
    in_sem, halo_send, halo_recv, x_send, x_recv, t_send, t_recv,
):
    _, bins, channels, windows = spectra.shape
    half = bins // 2
    middle = HMAX + STEP
    chunks = half // STEP
    fresh_chunks = (half - 2 * HMAX) // STEP
    first_edge_chunk = (half - HMAX) // STEP
    row_blocks = channels // ROWS
    scale = windows ** -0.5

    block = lax.axis_index("blk")
    block_count = lax.axis_size("blk")
    freq = lax.axis_index("freq")
    freq_count = lax.axis_size("freq")
    bin_total = bins * freq_count
    has_low = freq > 0
    has_high = freq < freq_count - 1

    partners = []
    mine = 0
    for round_index in range(ROUNDS):
        flip = block_count >> (round_index + 1)
        side = (block // flip) % 2
        partners.append(block + flip * (1 - 2 * side))
        mine = mine + side
    mine = mine % 2
    given = 1 - mine

    def chunk_start(which, chunk):
        return (half - STEP * (chunk + 1)) + which * (STEP * (2 * chunk + 1))

    def make_energy(k, first=0, last=row_blocks):
        @pl.loop(first, last)
        def _(block_index):
            rows = pl.ds(pl.multiple_of(block_index * ROWS, ROWS), ROWS)
            real_part = spectra[0, k, rows, :].astype(jnp.float32)
            imag_part = spectra[1, k, rows, :].astype(jnp.float32)
            energy[k + HMAX, rows, :] = real_part * real_part + imag_part * imag_part

    def whiten(k, first=0, last=row_blocks):
        position = freq * bins + k
        inside = []
        for offset in range(1, HMAX + 1):
            low = (position - offset >= 0).astype(jnp.int32)
            high = (position + offset < bin_total).astype(jnp.int32)
            inside.append((low + high).astype(jnp.float32))

        @pl.loop(first, last)
        def _(block_index):
            rows = pl.ds(pl.multiple_of(block_index * ROWS, ROWS), ROWS)
            width = widths[rows, :]
            counts = jnp.ones((ROWS, LANES), jnp.float32)
            weights = []
            for offset in range(1, HMAX + 1):
                weight = (width >= offset).astype(jnp.float32)
                counts = counts + weight * inside[offset - 1]
                weights.append(weight)
            inverse = 1.0 / counts
            for lane in range(0, windows, LANES):
                lanes = pl.ds(lane, LANES)
                smooth = energy[k + HMAX, rows, lanes]
                for offset in range(1, HMAX + 1):
                    pair = (
                        energy[k + HMAX - offset, rows, lanes]
                        + energy[k + HMAX + offset, rows, lanes]
                    )
                    smooth = smooth + weights[offset - 1] * pair
                factor = lax.rsqrt(jnp.maximum(smooth * inverse, 0.25))
                for part in range(2):
                    value = spectra[part, k, rows, lanes].astype(jnp.float32)
                    whitened[part, k, rows, lanes] = (value * factor).astype(jnp.bfloat16)

    def halo_copy(side):
        source = (HMAX, bins)[side]
        target = (bins + HMAX, 0)[side]
        return pltpu.make_async_remote_copy(
            src_ref=energy.at[pl.ds(source, HMAX)],
            dst_ref=energy.at[pl.ds(target, HMAX)],
            send_sem=halo_send.at[side],
            recv_sem=halo_recv.at[1 - side],
            device_id={"freq": freq + (2 * side - 1)},
            device_id_type=pl.DeviceIdType.MESH,
        )

    def spectra_copy(r, chunk, rows=pl.ds(0, channels)):
        return pltpu.make_async_remote_copy(
            src_ref=whitened.at[:, pl.ds(chunk_start(given, chunk), STEP), rows],
            dst_ref=taken.at[r, :, pl.ds(chunk * STEP, STEP), rows],
            send_sem=x_send.at[r, chunk],
            recv_sem=x_recv.at[r, chunk],
            device_id={"blk": partners[r]},
            device_id_type=pl.DeviceIdType.MESH,
        )

    def tile_copy(r, chunk, which):
        return pltpu.make_async_remote_copy(
            src_ref=sent_tiles.at[r, chunk],
            dst_ref=out.at[r, :, pl.ds(chunk_start(which, chunk), STEP)],
            send_sem=t_send.at[r, chunk],
            recv_sem=t_recv.at[r, chunk],
            device_id={"blk": partners[r]},
            device_id_type=pl.DeviceIdType.MESH,
        )

    def load(start, count, index, rows=pl.ds(0, channels)):
        span = pl.ds(start, count)
        return pltpu.make_async_copy(
            spectra_in.at[:, span, rows], spectra.at[:, span, rows], in_sem.at[index]
        )

    def piece_rows(piece):
        return pl.ds(pl.multiple_of(piece * (channels // PIECES), ROWS), channels // PIECES)

    def load_piece(piece):
        return load(half - middle, 2 * middle, piece, piece_rows(piece))

    for piece in range(PIECES):
        load_piece(piece).start()
    load_given = load(given * (half + middle), half - middle, PIECES)
    load_mine = load(mine * (half + middle), half - middle, PIECES + 1)
    load_given.start()
    load_mine.start()

    barrier = pltpu.get_barrier_semaphore()
    for partner in partners:
        pl.semaphore_signal(
            barrier, inc=1, device_id={"blk": partner}, device_id_type=pl.DeviceIdType.MESH
        )

    @pl.when(has_low)
    def _():
        pl.semaphore_signal(
            barrier, inc=1, device_id={"freq": freq - 1}, device_id_type=pl.DeviceIdType.MESH
        )

    @pl.when(has_high)
    def _():
        pl.semaphore_signal(
            barrier, inc=1, device_id={"freq": freq + 1}, device_id_type=pl.DeviceIdType.MESH
        )

    widths[...] = jnp.broadcast_to(
        widths_in[...].astype(jnp.float32), (channels, LANES)
    ).T

    def whiten_chunk(which, chunk):
        start = chunk_start(which, chunk)

        @pl.when(chunk < fresh_chunks)
        def _():
            for j in range(STEP):
                make_energy(start + j + HMAX * (2 * which - 1))

        @pl.when((chunk == first_edge_chunk) & (which == 0) & has_low)
        def _():
            halo_copy(1).wait_recv()

        @pl.when((chunk == first_edge_chunk) & (which == 1) & has_high)
        def _():
            halo_copy(0).wait_recv()

        for j in range(STEP):
            whiten(start + j)

    def give(chunk):
        for r in range(ROUNDS):
            spectra_copy(r, chunk).start()

    def first_piece(piece):
        first = piece * (row_blocks // PIECES)
        last = first + row_blocks // PIECES
        load_piece(piece).wait()

        @pl.loop(0, 2 * HMAX + STEP)
        def _(index):
            make_energy(half - HMAX - STEP * (1 - given) + index, first, last)

        for j in range(STEP):
            whiten(chunk_start(given, 0) + j, first, last)

    def give_piece(piece):
        for r in range(ROUNDS):
            spectra_copy(r, 0, piece_rows(piece)).start()

    first_piece(0)
    pl.semaphore_wait(barrier, ROUNDS + has_low.astype(jnp.int32) + has_high.astype(jnp.int32))
    give_piece(0)

    @pl.loop(1, PIECES)
    def _(piece):
        first_piece(piece)
        give_piece(piece)

    load_given.wait()
    load_mine.wait()

    @pl.loop(0, HMAX)
    def _(index):
        make_energy(index)
        make_energy(bins - HMAX + index)

    @pl.when(has_low)
    def _():
        halo_copy(0).start()

    @pl.when(jnp.logical_not(has_low))
    def _():
        energy[pl.ds(0, HMAX)] = jnp.zeros((HMAX, channels, windows), jnp.float32)

    @pl.when(has_high)
    def _():
        halo_copy(1).start()

    @pl.when(jnp.logical_not(has_high))
    def _():
        energy[pl.ds(bins + HMAX, HMAX)] = jnp.zeros((HMAX, channels, windows), jnp.float32)

    @pl.loop(1, chunks)
    def _(chunk):
        whiten_chunk(given, chunk)
        give(chunk)

    @pl.loop(0, chunks)
    def _(chunk):
        whiten_chunk(mine, chunk)

    @pl.loop(0, chunks)
    def _(chunk):
        start = chunk_start(mine, chunk)
        for r in range(ROUNDS):
            spectra_copy(r, chunk).wait_recv()

            @pl.loop(0, STEP)
            def _(j):
                own = jnp.concatenate([whitened[0, start + j], whitened[1, start + j]], axis=0)
                other = jnp.concatenate(
                    [taken[r, 0, chunk * STEP + j], taken[r, 1, chunk * STEP + j]], axis=0
                )
                both = lax.dot_general(
                    own, other, (((1,), (1,)), ((), ())), preferred_element_type=jnp.float32
                )
                real_sum = both[:channels, :channels] + both[channels:, channels:]
                imag_sum = both[channels:, :channels] - both[:channels, channels:]
                real_sum = real_sum * scale
                imag_sum = imag_sum * scale
                out[r, 0, start + j] = real_sum.astype(jnp.bfloat16)
                out[r, 1, start + j] = imag_sum.astype(jnp.bfloat16)
                sent_tiles[r, chunk, 0, j] = real_sum.T.astype(jnp.bfloat16)
                sent_tiles[r, chunk, 1, j] = (-imag_sum.T).astype(jnp.bfloat16)

            tile_copy(r, chunk, mine).start()

    @pl.when(has_low)
    def _():
        halo_copy(0).wait_send()

    @pl.when(has_high)
    def _():
        halo_copy(1).wait_send()

    @pl.loop(0, chunks)
    def _(chunk):
        for r in range(ROUNDS):
            spectra_copy(r, chunk).wait_send()
            tile_copy(r, chunk, mine).wait_send()
            tile_copy(r, chunk, given).wait_recv()


def per_device(spectra, halfwidth):
    _, bins, channels, windows = spectra.shape
    half = bins // 2
    chunks = half // STEP
    widths = halfwidth.reshape(1, channels)
    tiles = (ROUNDS, chunks, 2, STEP, channels, channels)
    dma = pltpu.SemaphoreType.DMA
    return pl.pallas_call(
        cross_kernel,
        out_shape=pltpu.VMEM((ROUNDS, 2, bins, channels, channels), jnp.bfloat16),
        in_specs=[
            pl.BlockSpec(memory_space=pltpu.HBM),
            pl.BlockSpec(memory_space=pltpu.VMEM),
        ],
        out_specs=pl.BlockSpec(memory_space=pltpu.VMEM),
        scratch_shapes=[
            pltpu.VMEM((2, bins, channels, windows), jnp.bfloat16),
            pltpu.VMEM((channels, LANES), jnp.float32),
            pltpu.VMEM((bins + 2 * HMAX, channels, windows), jnp.float32),
            pltpu.VMEM((2, bins, channels, windows), jnp.bfloat16),
            pltpu.VMEM((ROUNDS, 2, half, channels, windows), jnp.bfloat16),
            pltpu.VMEM(tiles, jnp.bfloat16),
            dma((PIECES + 2,)),
            dma((2,)),
            dma((2,)),
            dma((ROUNDS, chunks)),
            dma((ROUNDS, chunks)),
            dma((ROUNDS, chunks)),
            dma((ROUNDS, chunks)),
        ],
        compiler_params=pltpu.CompilerParams(
            collective_id=0, has_side_effects=True, vmem_limit_bytes=48 * 2**20
        ),
    )(spectra, widths)


def solution(mesh):
    return jax.shard_map(
        per_device,
        mesh=mesh,
        in_specs=(P(None, "freq", "blk", None), P("blk")),
        out_specs=P(None, None, "freq", "blk", None),
        check_vma=False,
    )
```

```python
import jax
import jax.numpy as jnp
from jax import lax
from jax.experimental import pallas as pl
from jax.experimental.pallas import tpu as pltpu
from jax.sharding import PartitionSpec as P

HMAX = 3
ROUNDS = 2
STEP = 2
PIECES = 4
ROWS = 16
LANES = 128


def cross_kernel(
    spectra_in, widths_in, out, spectra, widths, energy, whitened, taken, sent_tiles,
    in_sem, halo_send, halo_recv, x_send, x_recv, t_send, t_recv,
):
    _, bins, channels, windows = spectra.shape
    half = bins // 2
    middle = HMAX + STEP
    chunks = half // STEP
    fresh_chunks = (half - 2 * HMAX) // STEP
    first_edge_chunk = (half - HMAX) // STEP
    row_blocks = channels // ROWS
    scale = windows ** -0.5

    block = lax.axis_index("blk")
    block_count = lax.axis_size("blk")
    freq = lax.axis_index("freq")
    freq_count = lax.axis_size("freq")
    bin_total = bins * freq_count
    has_low = freq > 0
    has_high = freq < freq_count - 1

    partners = []
    mine = 0
    for round_index in range(ROUNDS):
        flip = block_count >> (round_index + 1)
        side = (block // flip) % 2
        partners.append(block + flip * (1 - 2 * side))
        mine = mine + side
    mine = mine % 2
    given = 1 - mine

    def chunk_start(which, chunk):
        return (half - STEP * (chunk + 1)) + which * (STEP * (2 * chunk + 1))

    def make_energy(k, first=0, last=row_blocks):
        @pl.loop(first, last)
        def _(block_index):
            rows = pl.ds(pl.multiple_of(block_index * ROWS, ROWS), ROWS)
            real_part = spectra[0, k, rows, :].astype(jnp.float32)
            imag_part = spectra[1, k, rows, :].astype(jnp.float32)
            energy[k + HMAX, rows, :] = real_part * real_part + imag_part * imag_part

    def whiten(k, first=0, last=row_blocks):
        position = freq * bins + k
        inside = []
        for offset in range(1, HMAX + 1):
            low = (position - offset >= 0).astype(jnp.int32)
            high = (position + offset < bin_total).astype(jnp.int32)
            inside.append((low + high).astype(jnp.float32))

        @pl.loop(first, last)
        def _(block_index):
            rows = pl.ds(pl.multiple_of(block_index * ROWS, ROWS), ROWS)
            width = widths[rows, :]
            counts = jnp.ones((ROWS, LANES), jnp.float32)
            weights = []
            for offset in range(1, HMAX + 1):
                weight = (width >= offset).astype(jnp.float32)
                counts = counts + weight * inside[offset - 1]
                weights.append(weight)
            inverse = 1.0 / counts
            for lane in range(0, windows, LANES):
                lanes = pl.ds(lane, LANES)
                smooth = energy[k + HMAX, rows, lanes]
                for offset in range(1, HMAX + 1):
                    pair = (
                        energy[k + HMAX - offset, rows, lanes]
                        + energy[k + HMAX + offset, rows, lanes]
                    )
                    smooth = smooth + weights[offset - 1] * pair
                factor = lax.rsqrt(jnp.maximum(smooth * inverse, 0.25))
                for part in range(2):
                    value = spectra[part, k, rows, lanes].astype(jnp.float32)
                    whitened[part, k, rows, lanes] = (value * factor).astype(jnp.bfloat16)

    def halo_copy(side):
        source = (HMAX, bins)[side]
        target = (bins + HMAX, 0)[side]
        return pltpu.make_async_remote_copy(
            src_ref=energy.at[pl.ds(source, HMAX)],
            dst_ref=energy.at[pl.ds(target, HMAX)],
            send_sem=halo_send.at[side],
            recv_sem=halo_recv.at[1 - side],
            device_id={"freq": freq + (2 * side - 1)},
            device_id_type=pl.DeviceIdType.MESH,
        )

    def spectra_copy(r, chunk, rows=pl.ds(0, channels)):
        return pltpu.make_async_remote_copy(
            src_ref=whitened.at[:, pl.ds(chunk_start(given, chunk), STEP), rows],
            dst_ref=taken.at[r, :, pl.ds(chunk * STEP, STEP), rows],
            send_sem=x_send.at[r, chunk],
            recv_sem=x_recv.at[r, chunk],
            device_id={"blk": partners[r]},
            device_id_type=pl.DeviceIdType.MESH,
        )

    def tile_copy(r, chunk, which):
        return pltpu.make_async_remote_copy(
            src_ref=sent_tiles.at[r, chunk],
            dst_ref=out.at[r, :, pl.ds(chunk_start(which, chunk), STEP)],
            send_sem=t_send.at[r, chunk],
            recv_sem=t_recv.at[r, chunk],
            device_id={"blk": partners[r]},
            device_id_type=pl.DeviceIdType.MESH,
        )

    def load(start, count, index, rows=pl.ds(0, channels)):
        span = pl.ds(start, count)
        return pltpu.make_async_copy(
            spectra_in.at[:, span, rows], spectra.at[:, span, rows], in_sem.at[index]
        )

    def piece_rows(piece):
        return pl.ds(pl.multiple_of(piece * (channels // PIECES), ROWS), channels // PIECES)

    def load_piece(piece):
        return load(half - middle, 2 * middle, piece, piece_rows(piece))

    for piece in range(PIECES):
        load_piece(piece).start()
    load_given = load(given * (half + middle), half - middle, PIECES)
    load_mine = load(mine * (half + middle), half - middle, PIECES + 1)
    load_given.start()
    load_mine.start()

    barrier = pltpu.get_barrier_semaphore()
    for partner in partners:
        pl.semaphore_signal(
            barrier, inc=1, device_id={"blk": partner}, device_id_type=pl.DeviceIdType.MESH
        )

    @pl.when(has_low)
    def _():
        pl.semaphore_signal(
            barrier, inc=1, device_id={"freq": freq - 1}, device_id_type=pl.DeviceIdType.MESH
        )

    @pl.when(has_high)
    def _():
        pl.semaphore_signal(
            barrier, inc=1, device_id={"freq": freq + 1}, device_id_type=pl.DeviceIdType.MESH
        )

    widths[...] = jnp.broadcast_to(
        widths_in[...].astype(jnp.float32), (channels, LANES)
    ).T

    def whiten_chunk(which, chunk):
        start = chunk_start(which, chunk)

        @pl.when(chunk < fresh_chunks)
        def _():
            for j in range(STEP):
                make_energy(start + j + HMAX * (2 * which - 1))

        @pl.when((chunk == first_edge_chunk) & (which == 0) & has_low)
        def _():
            halo_copy(1).wait_recv()

        @pl.when((chunk == first_edge_chunk) & (which == 1) & has_high)
        def _():
            halo_copy(0).wait_recv()

        for j in range(STEP):
            whiten(start + j)

    def give(chunk):
        for r in range(ROUNDS):
            spectra_copy(r, chunk).start()

    def first_piece(piece):
        first = piece * (row_blocks // PIECES)
        last = first + row_blocks // PIECES
        load_piece(piece).wait()

        @pl.loop(0, 2 * HMAX + STEP)
        def _(index):
            make_energy(half - HMAX - STEP * (1 - given) + index, first, last)

        for j in range(STEP):
            whiten(chunk_start(given, 0) + j, first, last)

    def give_piece(piece):
        for r in range(ROUNDS):
            spectra_copy(r, 0, piece_rows(piece)).start()

    first_piece(0)
    pl.semaphore_wait(barrier, ROUNDS + has_low.astype(jnp.int32) + has_high.astype(jnp.int32))
    give_piece(0)

    @pl.loop(1, PIECES)
    def _(piece):
        first_piece(piece)
        give_piece(piece)

    load_given.wait()
    load_mine.wait()

    @pl.loop(0, HMAX)
    def _(index):
        make_energy(index)
        make_energy(bins - HMAX + index)

    @pl.when(has_low)
    def _():
        halo_copy(0).start()

    @pl.when(jnp.logical_not(has_low))
    def _():
        energy[pl.ds(0, HMAX)] = jnp.zeros((HMAX, channels, windows), jnp.float32)

    @pl.when(has_high)
    def _():
        halo_copy(1).start()

    @pl.when(jnp.logical_not(has_high))
    def _():
        energy[pl.ds(bins + HMAX, HMAX)] = jnp.zeros((HMAX, channels, windows), jnp.float32)

    @pl.loop(1, chunks)
    def _(chunk):
        whiten_chunk(given, chunk)
        give(chunk)

    @pl.loop(0, chunks)
    def _(chunk):
        whiten_chunk(mine, chunk)

    @pl.loop(0, chunks)
    def _(chunk):
        start = chunk_start(mine, chunk)
        for r in range(ROUNDS):
            spectra_copy(r, chunk).wait_recv()

            @pl.loop(0, STEP)
            def _(j):
                own = jnp.concatenate([whitened[0, start + j], whitened[1, start + j]], axis=0)
                other = jnp.concatenate(
                    [taken[r, 0, chunk * STEP + j], taken[r, 1, chunk * STEP + j]], axis=0
                )
                both = lax.dot_general(
                    own, other, (((1,), (1,)), ((), ())), preferred_element_type=jnp.float32
                )
                real_sum = both[:channels, :channels] + both[channels:, channels:]
                imag_sum = both[channels:, :channels] - both[:channels, channels:]
                real_sum = real_sum * scale
                imag_sum = imag_sum * scale
                out[r, 0, start + j] = real_sum.astype(jnp.bfloat16)
                out[r, 1, start + j] = imag_sum.astype(jnp.bfloat16)
                sent_tiles[r, chunk, 0, j] = real_sum.T.astype(jnp.bfloat16)
                sent_tiles[r, chunk, 1, j] = (-imag_sum.T).astype(jnp.bfloat16)

            tile_copy(r, chunk, mine).start()

    @pl.when(has_low)
    def _():
        halo_copy(0).wait_send()

    @pl.when(has_high)
    def _():
        halo_copy(1).wait_send()

    @pl.loop(0, chunks)
    def _(chunk):
        for r in range(ROUNDS):
            spectra_copy(r, chunk).wait_send()
            tile_copy(r, chunk, mine).wait_send()
            tile_copy(r, chunk, given).wait_recv()


def store_kernel(tiles, out, sem):
    copies = [
        pltpu.make_async_copy(tiles.at[r, part], out.at[r, part], sem.at[r, part])
        for r in range(ROUNDS)
        for part in range(2)
    ]
    for copy in copies:
        copy.start()
    for copy in copies:
        copy.wait()


def per_device(spectra, halfwidth):
    _, bins, channels, windows = spectra.shape
    half = bins // 2
    chunks = half // STEP
    widths = halfwidth.reshape(1, channels)
    tiles = (ROUNDS, chunks, 2, STEP, channels, channels)
    dma = pltpu.SemaphoreType.DMA
    crossed = pl.pallas_call(
        cross_kernel,
        out_shape=pltpu.VMEM((ROUNDS, 2, bins, channels, channels), jnp.bfloat16),
        in_specs=[
            pl.BlockSpec(memory_space=pltpu.HBM),
            pl.BlockSpec(memory_space=pltpu.VMEM),
        ],
        out_specs=pl.BlockSpec(memory_space=pltpu.VMEM),
        scratch_shapes=[
            pltpu.VMEM((2, bins, channels, windows), jnp.bfloat16),
            pltpu.VMEM((channels, LANES), jnp.float32),
            pltpu.VMEM((bins + 2 * HMAX, channels, windows), jnp.float32),
            pltpu.VMEM((2, bins, channels, windows), jnp.bfloat16),
            pltpu.VMEM((ROUNDS, 2, half, channels, windows), jnp.bfloat16),
            pltpu.VMEM(tiles, jnp.bfloat16),
            dma((PIECES + 2,)),
            dma((2,)),
            dma((2,)),
            dma((ROUNDS, chunks)),
            dma((ROUNDS, chunks)),
            dma((ROUNDS, chunks)),
            dma((ROUNDS, chunks)),
        ],
        compiler_params=pltpu.CompilerParams(
            collective_id=0, has_side_effects=True, vmem_limit_bytes=48 * 2**20
        ),
    )(spectra, widths)
    return pl.pallas_call(
        store_kernel,
        out_shape=jax.ShapeDtypeStruct(crossed.shape, crossed.dtype),
        in_specs=[pl.BlockSpec(memory_space=pltpu.VMEM)],
        out_specs=pl.BlockSpec(memory_space=pltpu.HBM),
        scratch_shapes=[dma((ROUNDS, 2))],
    )(crossed)


def solution(mesh):
    return jax.shard_map(
        per_device,
        mesh=mesh,
        in_specs=(P(None, "freq", "blk", None), P("blk")),
        out_specs=P(None, None, "freq", "blk", None),
        check_vma=False,
    )
```
